32 devices in a mesh: rep: 8 (over y, x, core), shard: 4 (over z).
Axes of the slice: x: 2, y: 2, z: 4, core: 2. Of those that a mesh axis runs over, the one named last changes fastest.
Arguments:
- tokens: bfloat16 [4, 1024, 2048], P('shard', 'rep'), may hold values from -6 to 6
- teacher: bfloat16 [4, 1024, 2048], P('shard', 'rep'), may hold values from -6 to 6
- valid_mask: int32 [4, 1024], P('shard', 'rep'), may hold values from 0 to 1, as said below
- block_mask: int32 [4, 4, 4], P('shard'), may hold values 0 or 1
- routes: int32 [4, 1024, 4], P('shard', 'rep'), may hold values from 0 to 7, all different within a row; in each aligned block of 128 rows (0 to 127, 128 to 255, ..., all dimensions but the last counted through in order) at most 80 rows name the same one
- gates: float32 [4, 1024, 4], P('shard', 'rep'), may hold values from 0.3 to 1
- attn_gain: bfloat16 [2048], P('shard'), may hold values from 0.5 to 1.5
- w_qkv: bfloat16 [3, 2048, 2048], P(None, 'shard'), may hold values from -0.21875 to 0.21875
- qkv_bias: bfloat16 [3, 2048], P(None, 'shard'), may hold values from -3 to 3
- w_out: bfloat16 [2048, 2048], P('shard'), may hold values from -0.375 to 0.375
- ffn_gain: bfloat16 [2048], P('shard'), may hold values from 0.5 to 1.5
- shared_gate_up: bfloat16 [2, 2048, 5632], P(None, 'shard'), may hold values from -0.125 to 0.125
- shared_down: bfloat16 [5632, 2048], P('shard'), may hold values from -0.078125 to 0.078125
- shared_gate: bfloat16 [2048], P('shard'), may hold values from -0.125 to 0.125
- expert_gate_up: bfloat16 [8, 2, 2048, 1408], P('shard'), may hold values from -0.125 to 0.125
- expert_down: bfloat16 [8, 1408, 2048], P('shard'), may hold values from -0.15625 to 0.15625
Outputs:
- loss: float32 [], replicated
- block_out: bfloat16 [4, 1024, 2048], P('shard', 'rep')
- input_grad: float32 [4, 1024, 2048], P('shard', 'rep')
- attn_gain_grad: float32 [2048], P('shard')
- w_qkv_grad: float32 [3, 2048, 2048], P(None, 'shard', 'rep')
- qkv_bias_grad: float32 [3, 2048], P(None, 'shard')
- w_out_grad: float32 [2048, 2048], P('shard', 'rep')
- ffn_gain_grad: float32 [2048], P('shard')
- shared_gate_up_grad: float32 [2, 2048, 5632], P(None, 'shard', 'rep')
- shared_down_grad: float32 [5632, 2048], P('shard', 'rep')
- shared_gate_grad: float32 [2048], P('shard')
- expert_gate_up_grad: float32 [8, 2, 2048, 1408], P('shard', None, 'rep')
- expert_down_grad: float32 [8, 1408, 2048], P('shard', None, 'rep')
The draws below stay inside these ranges and needn't reach their ends.
Inputs may be any that keep to these rules, and one draw needn't show every extreme that they name: `routes`: each row names 4 different experts; in the 128 rows of one device no expert is named by more than 80 rows, a bound that some block reaches. `valid_mask`: 1 at every position of a sequence that is a multiple of 256.
All inputs are finite; a program needn't handle non-finite values. No bound on the sum of `block_mask` on one device may be relied on, other than what follows from the above.
Results may differ from the reference program's by a relative error of at most 0.025.
Values may be sent and summed in bfloat16 or wider, within the bound.
A program may use at most 704 MiB of HBM per device.

```python
import math
import jax
import jax.numpy as jnp
import numpy as np
from jax import lax

D = 2048
HEADS = 16
HD = 128
FE = 1408
SH = 5632
TOPK = 4
BLOCK = 256
TOK_DEV = 128
EXPERTS = 8
NSEQ = 4
LEN = 1024
TOKENS = 4096
NBLK = 4
CAP = 80


def draw_valid_mask(key, part):
    key = jax.random.fold_in(key, 7)
    places = jnp.arange(LEN, dtype=jnp.int32)
    level = 250 + 500 * places // LEN
    rolled = jax.random.randint(key, (NSEQ, LEN), 0, 1000, dtype=jnp.int32)
    keep = (rolled < level[None, :]) | (places % BLOCK == 0)[None, :]
    return keep.astype(jnp.int32)


def touch_ends(drawn, key, smallest, largest):
    longest = drawn.shape.index(max(drawn.shape))
    spots = []
    for shift in (0, 1):
        where = [jax.random.randint(jax.random.fold_in(key, axis), (), 0, length) for axis, length in enumerate(drawn.shape)]
        where[longest] = (where[longest] + shift) % drawn.shape[longest]
        spots.append(tuple(where))
    return drawn.at[spots[0]].set(smallest).at[spots[1]].set(largest)


def levels(stream_key, shape, pieces, low, largest):
    factor_of, own = 1.0, jax.random.fold_in(stream_key, 6)
    for axis_at, blocks in pieces:
        heights = jnp.exp(jax.random.uniform(jax.random.fold_in(own, axis_at), (blocks,), jnp.float32, low / len(pieces), largest / len(pieces)))
        factor_of = factor_of * jnp.repeat(heights, shape[axis_at] // blocks).reshape([-1 if axis == axis_at else 1 for axis in range(len(shape))])
    return factor_of


def assign_block(rng, own, number, rows, count, top, limit, lean):
    order = jax.random.permutation(rng, count)
    crowded, ordinary = shares(count, rows * top, limit, lean, True), shares(count, rows * top, limit, lean, False)
    places = jnp.arange(count)

    def named(tallies, offset_by):
        used = int((tallies > 0).sum())
        fixed = max(1, used // 4)
        moved = fixed + (places - fixed + offset_by * (used - fixed)) % max(1, count - fixed)
        return jnp.zeros((count,), jnp.int32).at[order[jnp.where(places < fixed, places, moved)]].set(jnp.asarray(tallies, jnp.int32))

    tallies = jnp.where(number % 4 == 0, named(crowded, number // 4), named(ordinary, number - number // 4 - 1))
    mixed = jax.random.permutation(jax.random.fold_in(own, 3), count)
    giver, receiver = mixed[0:count // 2 * 2:2], mixed[1:count // 2 * 2:2]
    room = jnp.minimum(tallies[giver] - 1, limit - tallies[receiver]) // 2
    room = jnp.where((giver == order[0]) | (receiver == order[0]) | (tallies[receiver] == 0), 0, jnp.maximum(room, 0))
    moved = jax.random.randint(jax.random.fold_in(own, 4), (count // 2,), 0, 1 << 20) % (room + 1)
    tallies = tallies.at[giver].add(-moved).at[receiver].add(moved)
    labels = jnp.searchsorted(jnp.cumsum(tallies), jnp.arange(rows * top), side="right").astype(jnp.int32)
    grid = labels.reshape(top, rows).T
    grid = grid[jax.random.permutation(jax.random.fold_in(own, 1), rows)]
    offset_by = jax.random.randint(jax.random.fold_in(own, 2), (rows, 1), 0, top)
    return jnp.take_along_axis(grid, (jnp.arange(top)[None, :] + offset_by) % top, axis=1)


def shares(count, total, most, skew, full):
    loads = [(1 << 20) // math.isqrt(standing ** skew) + 1 for standing in range(1, count + 1)]
    largest = most if full else min(most, max(-(-total // count), total * loads[0] // sum(loads)))
    least = 1 if total - largest >= count - 1 else 0
    holding, surplus = [largest] + [least] * (count - 1), total - largest - least * (count - 1)
    while surplus > 0:
        candidates = [i for i in range(1, count) if holding[i] < largest] or [i for i in range(1, count) if holding[i] < most]
        pool, budget = sum([loads[i] for i in candidates]), surplus
        for i in candidates:
            addition = min(most - holding[i], max(1, budget * loads[i] // pool), surplus)
            holding[i] = holding[i] + addition
            surplus = surplus - addition
    return np.array(holding)


def bell_draw(own_key, extent, scale, reach, split=(), held_as=jnp.bfloat16):
    array = scale * jax.random.normal(own_key, extent, jnp.float32)
    if split:
        array = array * levels(own_key, extent, split, -0.22, 0.18)
    return jnp.clip(array, -reach, reach).astype(held_as)


def setup_inputs(seed: int = 0) -> dict:
    key_list = jax.random.split(jax.random.key(seed), 17)
    tokens = bell_draw(key_list[0], (NSEQ, LEN, D), 1.0, 6.0, ((0, 4), (1, 8)))
    teacher = bell_draw(key_list[1], (NSEQ, LEN, D), 1.0, 6.0, ((0, 4), (1, 8)))
    valid_mask = draw_valid_mask(jax.random.fold_in(key_list[16], 71), 0)
    block_mask = touch_ends((jax.random.randint(key_list[3], (NSEQ, NBLK, NBLK), 0, 4) < 3).astype(jnp.int32), jax.random.fold_in(key_list[3], 1), 0, 1)
    routes_keys = jax.random.split(jax.random.fold_in(key_list[4], 1), NSEQ * LEN // TOK_DEV)
    routes_turns = jax.random.permutation(jax.random.fold_in(key_list[4], 3), NSEQ * LEN // TOK_DEV)
    routes = jax.vmap(lambda own, number: assign_block(jax.random.fold_in(key_list[4], 2), own, number, TOK_DEV, EXPERTS, TOPK, CAP, 1))(routes_keys, routes_turns).reshape((NSEQ, LEN, TOPK))
    gates = jnp.clip(jnp.exp(math.log(1.0) - 1.2039728 * jax.random.uniform(key_list[5], (NSEQ, LEN, TOPK), jnp.float32) ** levels(key_list[5], (NSEQ, LEN, TOPK), ((0, 4), (1, 8)), -0.2, 0.2)), 0.3, 1.0)
    attn_gain = jnp.clip(1.0 + 0.1 * jax.random.normal(key_list[6], (D,), jnp.float32), 0.5, 1.5).astype(jnp.bfloat16)
    w_qkv = bell_draw(key_list[7], (3, D, HEADS * HD), (D * 2 // 5) ** -0.5, 0.21875, ((1, 4),))
    qkv_bias = bell_draw(key_list[8], (3, HEADS * HD), 0.5, 3.0, ((1, 4),))
    w_out = bell_draw(key_list[9], (HEADS * HD, D), (HEADS * HD // 8) ** -0.5, 0.375, ((0, 4),))
    ffn_gain = jnp.clip(1.0 + 0.1 * jax.random.normal(key_list[10], (D,), jnp.float32), 0.5, 1.5).astype(jnp.bfloat16)
    shared_gate_up = bell_draw(key_list[11], (2, D, SH), D ** -0.5, 0.125, ((1, 4),))
    shared_down = bell_draw(key_list[12], (SH, D), SH ** -0.5, 0.078125, ((0, 4),))
    shared_gate = bell_draw(key_list[13], (D,), D ** -0.5, 0.125, ((0, 4),))
    expert_gate_up = bell_draw(key_list[14], (EXPERTS, 2, D, FE), D ** -0.5, 0.125, ((0, 4),))
    expert_down = bell_draw(key_list[15], (EXPERTS, FE, D), FE ** -0.5, 0.15625, ((0, 4),))
    return dict(tokens=tokens, teacher=teacher, valid_mask=valid_mask, block_mask=block_mask, routes=routes, gates=gates, attn_gain=attn_gain, w_qkv=w_qkv, qkv_bias=qkv_bias, w_out=w_out, ffn_gain=ffn_gain, shared_gate_up=shared_gate_up, shared_down=shared_down, shared_gate=shared_gate, expert_gate_up=expert_gate_up, expert_down=expert_down)


EPS = 1e-06
THETA = 1000000.0
NEG = -1e+30
QUERY_SPAN = 512
HIGH = lax.Precision.HIGHEST

@jax.custom_vjp
def low(v):
    return lax.optimization_barrier(v.astype(jnp.bfloat16)).astype(jnp.float32)

@jax.custom_vjp
def low_back(v):
    return v

def low_keep(v):
    return (low(v), None)

def low_pass(kept, grad):
    return (grad,)

def back_keep(v):
    return (v, None)

def back_low(kept, grad):
    return (low(grad),)
low.defvjp(low_keep, low_pass)
low_back.defvjp(back_keep, back_low)

def norm_rows(values, gain_vec):
    return values * lax.rsqrt(lax.optimization_barrier(jnp.mean(values * values, axis=-1, keepdims=True)) + EPS) * gain_vec

def rope_tables(offset, count, width):
    half_width = width // 2
    feature = jnp.arange(half_width, dtype=jnp.int32).astype(jnp.float32)
    frequency = THETA ** (-2.0 * feature / width)
    places = (offset + jnp.arange(count, dtype=jnp.int32)).astype(jnp.float32)
    angles = places[:, None] * frequency[None, :]
    angles = jnp.concatenate([angles, angles], axis=1)
    return (jnp.cos(angles), jnp.sin(angles))

def rotate(values, cosine_table, sine_table, head_count):
    row_count = values.shape[0]
    shaped = values.reshape(row_count, head_count, -1)
    half_width = shaped.shape[-1] // 2
    turned = jnp.concatenate([-shaped[..., half_width:], shaped[..., :half_width]], axis=-1)
    return (shaped * cosine_table[:, None, :] + turned * sine_table[:, None, :]).reshape(row_count, -1)

def attention(query, keys, values, block_table):
    length = query.shape[0]
    query_len = min(QUERY_SPAN, length)
    key_heads = keys.reshape(length, HEADS, HD)
    value_heads = values.reshape(length, HEADS, HD)
    key_blocks = jnp.arange(length, dtype=jnp.int32) // BLOCK
    score_scale = 1.0 / math.sqrt(HD)

    def one_block(block_item):
        query_part, query_first = block_item
        query_blocks = (query_first + jnp.arange(query_len, dtype=jnp.int32)) // BLOCK
        raw_scores = jnp.einsum('qhd,khd->hqk', query_part, key_heads, precision=HIGH) * score_scale
        scores = low_back(raw_scores)
        table_rows = jnp.take(block_table, query_blocks, axis=0)
        chosen = jnp.take(table_rows, key_blocks, axis=1)
        earlier = (key_blocks[None, :] < query_blocks[:, None]) & (chosen == 1)
        permitted = earlier | (key_blocks[None, :] == query_blocks[:, None])
        masked = jnp.where(permitted[None], scores, NEG)
        row_peak = lax.optimization_barrier(jnp.max(masked, axis=-1, keepdims=True))
        exp_terms = jnp.exp(masked - row_peak)
        probs = low(exp_terms / lax.optimization_barrier(jnp.sum(exp_terms, axis=-1, keepdims=True)))
        return jnp.einsum('hqk,khd->qhd', probs, value_heads, precision=HIGH)
    query_parts = query.reshape(length // query_len, query_len, HEADS, HD)
    starts = jnp.arange(length // query_len, dtype=jnp.int32) * query_len
    outputs = lax.map(jax.checkpoint(one_block), (query_parts, starts))
    return outputs.reshape(length, HEADS, HD)

def layer_seq(inputs, weights, teach, valid, route_rows, gate_rows, block_table, loss_scaling):
    attn_gain, w_qkv, qkv_bias, w_out, ffn_gain, shared_gate_up, shared_down, shared_gate, expert_gate_up, expert_down = weights
    length = inputs.shape[0]
    normed_in = low(norm_rows(inputs, attn_gain))
    projected = low_back(jnp.einsum('ld,jdf->jlf', normed_in, w_qkv, precision=HIGH) + qkv_bias[:, None, :])
    cosine_table, sine_table = rope_tables(0, length, HD)
    query = low(rotate(projected[0], cosine_table, sine_table, HEADS))
    keys = low(rotate(projected[1], cosine_table, sine_table, HEADS))
    values = low(projected[2])
    attended = attention(query, keys, values, block_table)
    attended_low = low(low_back(attended)).reshape(length, HEADS * HD)
    mid = inputs + low_back(jnp.dot(attended_low, w_out, precision=HIGH))
    normed_mid = low(norm_rows(mid, ffn_gain))
    shared_pre = low_back(jnp.einsum('ld,jdf->jlf', normed_mid, shared_gate_up, precision=HIGH))
    shared_hidden = low(jax.nn.silu(shared_pre[0]) * shared_pre[1])
    shared_out = low_back(jnp.dot(shared_hidden, shared_down, precision=HIGH))
    shared_weight = jax.nn.sigmoid(jnp.dot(normed_mid, shared_gate, precision=HIGH))
    mixed = shared_weight[:, None] * shared_out
    expert_ids = jnp.arange(EXPERTS, dtype=jnp.int32)
    chosen = (route_rows[:, :, None] == expert_ids[None, None, :]).astype(gate_rows.dtype)
    route_weight = lax.optimization_barrier(jnp.sum(gate_rows[:, :, None] * chosen, axis=1))
    for expert in range(EXPERTS):
        expert_in = low_back(normed_mid)
        expert_pre = low_back(jnp.einsum('ld,jdf->jlf', expert_in, expert_gate_up[expert], precision=HIGH))
        expert_hidden = low(jax.nn.silu(expert_pre[0]) * expert_pre[1])
        expert_out = low(low_back(jnp.dot(expert_hidden, expert_down[expert], precision=HIGH)))
        mixed = mixed + route_weight[:, expert:expert + 1] * expert_out
    outputs = mid + mixed
    diff_rows = outputs - teach
    squared = jnp.sum(valid * lax.optimization_barrier(jnp.sum(diff_rows * diff_rows, axis=1))) * loss_scaling
    return (squared, outputs)

def reference(tokens, teacher, valid_mask, block_mask, routes, gates, attn_gain, w_qkv, qkv_bias, w_out, ffn_gain, shared_gate_up, shared_down, shared_gate, expert_gate_up, expert_down):
    weights = tuple((member.astype(jnp.float32) for member in (attn_gain, w_qkv, qkv_bias, w_out, ffn_gain, shared_gate_up, shared_down, shared_gate, expert_gate_up, expert_down)))
    valid_float = valid_mask.astype(jnp.float32)
    count = jnp.sum(valid_float)
    loss_scaling = 1.0 / (count * D)
    seed_value = TOKENS * D / 4.0

    def per_seq(carried, seq_item):
        loss_sum, grad_sums = carried
        inputs, teach, valid, block_table, route_rows, gate_rows = seq_item

        def forward(inputs_float, *weights_float):
            return layer_seq(inputs_float, weights_float, teach, valid, route_rows, gate_rows, block_table, loss_scaling)
        squared, pull, outputs = jax.vjp(forward, inputs.astype(jnp.float32), *weights, has_aux=True)
        gradient = pull(jnp.ones_like(squared) * seed_value)
        new_sums = tuple((held + fresh for held, fresh in zip(grad_sums, gradient[1:])))
        return ((loss_sum + squared, new_sums), (outputs.astype(jnp.bfloat16), gradient[0]))
    start_carry = (jnp.zeros((), jnp.float32), tuple((jnp.zeros_like(member) for member in weights)))
    (loss_total, grad_total), (block_out, input_grad) = lax.scan(per_seq, start_carry, (tokens, teacher.astype(jnp.float32), valid_float, block_mask, routes, gates))
    return (loss_total, block_out, input_grad, grad_total[0], grad_total[1], grad_total[2], grad_total[3], grad_total[4], grad_total[5], grad_total[6], grad_total[7], grad_total[8], grad_total[9])
```

```python
import math

import jax
import jax.numpy as jnp
from jax import lax
from jax.sharding import PartitionSpec as P

HEADS = 16
HD = 128
BLOCK = 256
CAP = 80


EPS = 1e-06
THETA = 1000000.0
NEG = -1e30
KEY_SPAN = 1024


def norm_scale(values):
    return lax.rsqrt(jnp.mean(values * values, axis=-1, keepdims=True) + EPS)


def norm_back(values, gain_vec, grad_out):
    scaling = norm_scale(values)
    normed = values * scaling
    d_normed = grad_out * gain_vec
    d_gain = jnp.sum(grad_out * normed, axis=0)
    d_values = scaling * (d_normed - normed * jnp.mean(d_normed * normed, axis=-1, keepdims=True))
    return (d_values, d_gain)


def rope_tables(offset, count, width):
    half_width = width // 2
    feature = jnp.arange(half_width, dtype=jnp.int32).astype(jnp.float32)
    frequency = THETA ** (-2.0 * feature / width)
    places = (offset + jnp.arange(count, dtype=jnp.int32)).astype(jnp.float32)
    angles = places[:, None] * frequency[None, :]
    angles = jnp.concatenate([angles, angles], axis=1)
    return (jnp.cos(angles), jnp.sin(angles))


def rotate(values, cosine_table, sine_table, head_count):
    row_count = values.shape[0]
    shaped = values.reshape(row_count, head_count, -1)
    half_width = shaped.shape[-1] // 2
    turned = jnp.concatenate([-shaped[..., half_width:], shaped[..., :half_width]], axis=-1)
    return (shaped * cosine_table[:, None, :] + turned * sine_table[:, None, :]).reshape(
        row_count, -1
    )


def rotate_back(gradient, cosine_table, sine_table, head_count):
    row_count = gradient.shape[0]
    shaped = gradient.reshape(row_count, head_count, -1)
    half_width = shaped.shape[-1] // 2
    sine_part = shaped * sine_table[:, None, :]
    turned = jnp.concatenate([sine_part[..., half_width:], -sine_part[..., :half_width]], axis=-1)
    return (shaped * cosine_table[:, None, :] + turned).reshape(row_count, -1)


def swiglu(gate_part, up_part):
    return jax.nn.silu(gate_part) * up_part


def swiglu_grads(gate_part, up_part, d_hidden):
    sigmoid_val = jax.nn.sigmoid(gate_part)
    d_gate = d_hidden * up_part * sigmoid_val * (1.0 + gate_part * (1.0 - sigmoid_val))
    d_up_part = d_hidden * gate_part * sigmoid_val
    return (d_gate, d_up_part)


def keep_state(carried):
    return carried


def allowed_keys(block_table, query_first, query_count, key_first, key_count, block_len):
    query_blocks = (query_first + jnp.arange(query_count, dtype=jnp.int32)) // block_len
    key_blocks = (key_first + jnp.arange(key_count, dtype=jnp.int32)) // block_len
    table_rows = jnp.take(block_table, query_blocks, axis=0)
    chosen = jnp.take(table_rows, key_blocks, axis=1)
    earlier = (key_blocks[None, :] < query_blocks[:, None]) & (chosen == 1)
    return earlier | (key_blocks[None, :] == query_blocks[:, None])


def expert_forward(inputs, gate_up_weight, down_weight):
    pre_act = jnp.einsum(
        "sgcd,gjdf->sgcjf", inputs, gate_up_weight, preferred_element_type=jnp.float32
    )
    hidden = swiglu(pre_act[..., 0, :], pre_act[..., 1, :]).astype(jnp.bfloat16)
    outputs = jnp.einsum("sgcf,gfd->sgcd", hidden, down_weight, preferred_element_type=jnp.float32)
    return (outputs.astype(jnp.bfloat16), pre_act)


def expert_input_grads(pre_act, d_outputs, gate_up_weight, down_weight):
    d_hidden = jnp.einsum(
        "sgcd,gfd->sgcf", d_outputs, down_weight, preferred_element_type=jnp.float32
    )
    d_gate, d_up_part = swiglu_grads(pre_act[..., 0, :], pre_act[..., 1, :], d_hidden)
    d_pre = jnp.stack([d_gate, d_up_part], axis=-2).astype(jnp.bfloat16)
    d_inputs = jnp.einsum(
        "sgcjf,gjdf->sgcd", d_pre, gate_up_weight, preferred_element_type=jnp.float32
    )
    return (d_inputs.astype(jnp.bfloat16), d_pre)


def expert_weight_grads(inputs, pre_act, d_pre, d_outputs):
    hidden = swiglu(pre_act[..., 0, :], pre_act[..., 1, :]).astype(jnp.bfloat16)
    d_gate_up = jnp.einsum("sgcd,sgcjf->gjdf", inputs, d_pre, preferred_element_type=jnp.float32)
    d_down = jnp.einsum("sgcf,sgcd->gfd", hidden, d_outputs, preferred_element_type=jnp.float32)
    return (d_gate_up, d_down)


def per_device(
    tokens,
    teacher,
    valid_mask,
    block_mask,
    routes,
    gates,
    attn_gain,
    w_qkv,
    qkv_bias,
    w_out,
    ffn_gain,
    shared_gate_up,
    shared_down,
    shared_gate,
    expert_gate_up,
    expert_down,
):
    x_rows = tokens[0].astype(jnp.float32)
    row_count = x_rows.shape[0]
    model_width = x_rows.shape[1]
    groups = lax.axis_size("shard")
    replicas = lax.axis_size("rep")
    local_experts = expert_gate_up.shape[0]
    experts_total = groups * local_experts
    first_row = lax.axis_index("rep") * row_count
    last_row = first_row + row_count - 1
    seq_len = row_count * replicas
    key_len = min(KEY_SPAN, seq_len)
    key_count = seq_len // key_len
    score_scale = 1.0 / math.sqrt(HD)
    block_table = block_mask[0]
    attn_gain_all, qkv_all, bias_all, out_weight_all = (
        lax.all_gather(attn_gain, "shard", axis=0, tiled=True),
        lax.all_gather(w_qkv, "shard", axis=1, tiled=True),
        lax.all_gather(qkv_bias, "shard", axis=1, tiled=True),
        lax.all_gather(w_out, "shard", axis=0, tiled=True),
    )
    attn_gain_float = attn_gain_all.astype(jnp.float32)
    normed_low = (x_rows * norm_scale(x_rows) * attn_gain_float).astype(jnp.bfloat16)
    projected = jnp.einsum("ld,jdf->jlf", normed_low, qkv_all, preferred_element_type=jnp.float32)
    projected = projected + bias_all.astype(jnp.float32)[:, None, :]
    cosine_table, sine_table = rope_tables(first_row, row_count, HD)
    query_low = rotate(projected[0], cosine_table, sine_table, HEADS).astype(jnp.bfloat16)
    key_low = rotate(projected[1], cosine_table, sine_table, HEADS).astype(jnp.bfloat16)
    value_low = projected[2].astype(jnp.bfloat16)
    all_keys, all_values = (
        lax.all_gather(key_low, "rep", axis=0, tiled=True),
        lax.all_gather(value_low, "rep", axis=0, tiled=True),
    )
    query_heads = query_low.reshape(row_count, HEADS, HD)

    def block_scores(block_index):
        key_first = block_index * key_len
        key_part = lax.dynamic_slice_in_dim(all_keys, key_first, key_len, 0).reshape(
            key_len, HEADS, HD
        )
        value_part = lax.dynamic_slice_in_dim(all_values, key_first, key_len, 0).reshape(
            key_len, HEADS, HD
        )
        raw_scores = (
            jnp.einsum("qhd,khd->hqk", query_heads, key_part, preferred_element_type=jnp.float32)
            * score_scale
        )
        permitted = allowed_keys(block_table, first_row, row_count, key_first, key_len, BLOCK)[None]
        masked = jnp.where(permitted, raw_scores, NEG)
        return (masked, permitted, key_part, value_part)

    def lse_step(block_index, carried):

        def lse_live_block(running):
            run_max, run_total = running
            masked, permitted, key_part, value_part = block_scores(block_index)
            new_max = jnp.maximum(run_max, jnp.max(masked, axis=-1))
            weights = jnp.where(permitted, jnp.exp(masked - new_max[..., None]), 0.0)
            return (new_max, run_total * jnp.exp(run_max - new_max) + jnp.sum(weights, axis=-1))

        return lax.cond(block_index * key_len <= last_row, lse_live_block, keep_state, carried)

    start_stats = (
        jnp.full((HEADS, row_count), NEG, jnp.float32),
        jnp.zeros((HEADS, row_count), jnp.float32),
    )
    run_max, run_total = lax.fori_loop(0, key_count, lse_step, start_stats)
    log_total = run_max + jnp.log(run_total)

    def probs_of(masked, permitted):
        return jnp.where(permitted, jnp.exp(masked - log_total[..., None]), 0.0)

    def output_step(block_index, partial_out):

        def output_live_block(running):
            masked, permitted, key_part, value_part = block_scores(block_index)
            weights_low = probs_of(masked, permitted).astype(jnp.bfloat16)
            return running + jnp.einsum(
                "hqk,khd->qhd", weights_low, value_part, preferred_element_type=jnp.float32
            )

        return lax.cond(
            block_index * key_len <= last_row, output_live_block, keep_state, partial_out
        )

    attended = lax.fori_loop(
        0, key_count, output_step, jnp.zeros((row_count, HEADS, HD), jnp.float32)
    )
    attended_low = attended.reshape(row_count, HEADS * HD).astype(jnp.bfloat16)
    mid_rows = x_rows + jnp.dot(attended_low, out_weight_all, preferred_element_type=jnp.float32)
    ffn_gain_all, shared_gate_up_all, shared_down_all, shared_gate_all = (
        lax.all_gather(ffn_gain, "shard", axis=0, tiled=True),
        lax.all_gather(shared_gate_up, "shard", axis=1, tiled=True),
        lax.all_gather(shared_down, "shard", axis=0, tiled=True),
        lax.all_gather(shared_gate, "shard", axis=0, tiled=True),
    )
    ffn_gain_float = ffn_gain_all.astype(jnp.float32)
    normed_mid = (mid_rows * norm_scale(mid_rows) * ffn_gain_float).astype(jnp.bfloat16)
    shared_pre = jnp.einsum(
        "ld,jdf->jlf", normed_mid, shared_gate_up_all, preferred_element_type=jnp.float32
    )
    shared_hidden = swiglu(shared_pre[0], shared_pre[1]).astype(jnp.bfloat16)
    shared_out = jnp.dot(shared_hidden, shared_down_all, preferred_element_type=jnp.float32)
    shared_weight = jax.nn.sigmoid(
        jnp.dot(normed_mid, shared_gate_all, preferred_element_type=jnp.float32)
    )
    route_rows = routes[0]
    gate_rows = gates[0]
    top_count = route_rows.shape[1]
    flat_expert = route_rows.reshape(-1)
    one_hot = (flat_expert[:, None] == jnp.arange(experts_total, dtype=jnp.int32)[None, :]).astype(
        jnp.int32
    )
    flat_slot = jnp.sum((jnp.cumsum(one_hot, axis=0) - one_hot) * one_hot, axis=1)
    flat_token = jnp.arange(row_count * top_count, dtype=jnp.int32) // top_count
    slot_token = (
        jnp.zeros((experts_total, CAP), jnp.int32).at[flat_expert, flat_slot].set(flat_token)
    )
    token_buffer = normed_mid[slot_token]
    received = lax.all_to_all(token_buffer, "shard", split_axis=0, concat_axis=0, tiled=True)
    shaped = received.reshape(groups, local_experts, received.shape[1], received.shape[2])
    outputs, pre_act = expert_forward(shaped, expert_gate_up, expert_down)
    sent_out = outputs.reshape(received.shape)
    pre_remote = pre_act.reshape(received.shape[0], received.shape[1], 2, -1)
    expert_buffer = lax.all_to_all(sent_out, "shard", split_axis=0, concat_axis=0, tiled=True)
    picked = expert_buffer[flat_expert, flat_slot].reshape(row_count, top_count, model_width)
    expert_mix = jnp.sum(gate_rows[:, :, None] * picked.astype(jnp.float32), axis=1)
    out_rows = mid_rows + shared_weight[:, None] * shared_out + expert_mix
    diff_rows = out_rows - teacher[0].astype(jnp.float32)
    valid_rows = valid_mask[0].astype(jnp.float32)
    squares_local = jnp.sum(valid_rows * jnp.sum(diff_rows * diff_rows, axis=1))
    count_local = jnp.sum(valid_rows)
    squares_total, count_total = lax.psum((squares_local, count_local), ("rep", "shard"))
    loss_value = squares_total / (count_total * model_width)
    tokens_all = row_count * replicas * groups
    d_rows = valid_rows[:, None] * diff_rows * (tokens_all / (2.0 * count_total))
    d_shared_out = (shared_weight[:, None] * d_rows).astype(jnp.bfloat16)
    d_shared_hidden = jnp.einsum(
        "ld,fd->lf", d_shared_out, shared_down_all, preferred_element_type=jnp.float32
    )
    d_shared_down = jnp.einsum(
        "lf,ld->fd", shared_hidden, d_shared_out, preferred_element_type=jnp.float32
    )
    d_logit = jnp.sum(shared_out * d_rows, axis=1) * shared_weight * (1.0 - shared_weight)
    d_shared_gate = jnp.einsum("l,ld->d", d_logit, normed_mid.astype(jnp.float32))
    d_gate_shared, d_up_shared = swiglu_grads(shared_pre[0], shared_pre[1], d_shared_hidden)
    d_shared_pre = jnp.stack([d_gate_shared, d_up_shared]).astype(jnp.bfloat16)
    d_shared_gate_up = jnp.einsum(
        "ld,jlf->jdf", normed_mid, d_shared_pre, preferred_element_type=jnp.float32
    )
    d_normed_mid = jnp.einsum(
        "jlf,jdf->ld", d_shared_pre, shared_gate_up_all, preferred_element_type=jnp.float32
    )
    d_normed_mid = d_normed_mid + d_logit[:, None] * shared_gate_all.astype(jnp.float32)[None, :]
    d_picked = (gate_rows[:, :, None] * d_rows[:, None, :]).astype(jnp.bfloat16)
    d_picked = d_picked.reshape(row_count * top_count, model_width)
    d_buffer = (
        jnp.zeros((experts_total, CAP, model_width), jnp.bfloat16)
        .at[flat_expert, flat_slot]
        .set(d_picked)
    )
    d_remote = lax.all_to_all(d_buffer, "shard", split_axis=0, concat_axis=0, tiled=True)
    lead_shape = (groups, local_experts, d_remote.shape[1])
    pre_shaped = pre_remote.reshape(lead_shape + pre_remote.shape[2:])
    d_shaped = d_remote.reshape(lead_shape + d_remote.shape[2:])
    d_inputs_remote, d_pre_remote = expert_input_grads(
        pre_shaped, d_shaped, expert_gate_up, expert_down
    )
    d_token_buffer = lax.all_to_all(
        d_inputs_remote.reshape(d_remote.shape), "shard", split_axis=0, concat_axis=0, tiled=True
    )
    inputs_shaped = received.reshape(lead_shape + received.shape[2:])
    d_expert_gate_up, d_expert_down = expert_weight_grads(
        inputs_shaped, pre_shaped, d_pre_remote, d_shaped
    )
    d_from_experts = d_token_buffer[flat_expert, flat_slot].astype(jnp.float32)
    d_from_experts = jnp.sum(d_from_experts.reshape(row_count, top_count, model_width), axis=1)
    d_normed_mid = d_normed_mid + d_from_experts
    d_mid_norm, d_ffn_gain = norm_back(mid_rows, ffn_gain_float, d_normed_mid)
    d_mid = d_rows + d_mid_norm
    d_branch = d_mid.astype(jnp.bfloat16)
    d_out_weight = jnp.einsum(
        "lf,ld->fd", attended_low, d_branch, preferred_element_type=jnp.float32
    )
    d_attended = jnp.einsum(
        "ld,fd->lf", d_branch, out_weight_all, preferred_element_type=jnp.float32
    )
    d_attended = d_attended.astype(jnp.bfloat16).reshape(row_count, HEADS, HD)
    delta_rows = jnp.einsum("qhd,qhd->hq", d_attended.astype(jnp.float32), attended)

    def grad_step(block_index, carried):

        def grad_live_block(running):
            d_query, d_keys, d_values = running
            key_first = block_index * key_len
            masked, permitted, key_part, value_part = block_scores(block_index)
            weights_full = probs_of(masked, permitted)
            d_value_part = jnp.einsum(
                "hqk,qhd->khd",
                weights_full.astype(jnp.bfloat16),
                d_attended,
                preferred_element_type=jnp.float32,
            )
            d_weights = jnp.einsum(
                "qhd,khd->hqk", d_attended, value_part, preferred_element_type=jnp.float32
            )
            d_scores = (weights_full * (d_weights - delta_rows[..., None])).astype(jnp.bfloat16)
            d_query = d_query + jnp.einsum(
                "hqk,khd->qhd", d_scores, key_part, preferred_element_type=jnp.float32
            )
            d_key_part = (
                jnp.einsum(
                    "hqk,qhd->khd", d_scores, query_heads, preferred_element_type=jnp.float32
                )
                * score_scale
            )
            d_keys = lax.dynamic_update_slice_in_dim(
                d_keys, d_key_part.reshape(key_len, -1), key_first, 0
            )
            d_values = lax.dynamic_update_slice_in_dim(
                d_values, d_value_part.reshape(key_len, -1), key_first, 0
            )
            return (d_query, d_keys, d_values)

        return lax.cond(block_index * key_len <= last_row, grad_live_block, keep_state, carried)

    zero_keys = jnp.zeros((seq_len, HEADS * HD), jnp.float32)
    start_grads = (jnp.zeros((row_count, HEADS, HD), jnp.float32), zero_keys, zero_keys)
    d_query, d_keys, d_values = lax.fori_loop(0, key_count, grad_step, start_grads)
    own_keys, own_values = (
        lax.psum_scatter(
            d_keys.astype(jnp.bfloat16), "rep", scatter_dimension=0, tiled=True
        ).astype(jnp.float32),
        lax.psum_scatter(
            d_values.astype(jnp.bfloat16), "rep", scatter_dimension=0, tiled=True
        ).astype(jnp.float32),
    )
    d_projected = jnp.stack(
        [
            rotate_back(
                d_query.reshape(row_count, -1) * score_scale, cosine_table, sine_table, HEADS
            ),
            rotate_back(own_keys, cosine_table, sine_table, HEADS),
            own_values,
        ]
    ).astype(jnp.bfloat16)
    d_qkv = jnp.einsum("ld,jlf->jdf", normed_low, d_projected, preferred_element_type=jnp.float32)
    d_bias = jnp.sum(d_projected.astype(jnp.float32), axis=1)
    d_normed_in = jnp.einsum(
        "jlf,jdf->ld", d_projected, qkv_all, preferred_element_type=jnp.float32
    )
    d_x_norm, d_attn_gain = norm_back(x_rows, attn_gain_float, d_normed_in)
    d_input_rows = d_mid + d_x_norm
    (
        part_attn_gain,
        part_qkv,
        part_bias,
        part_out,
        part_ffn_gain,
        part_shared_gate_up,
        part_shared_down,
        part_shared_gate,
    ) = (
        lax.psum_scatter(
            d_attn_gain.astype(jnp.bfloat16), "shard", scatter_dimension=0, tiled=True
        ).astype(jnp.float32),
        lax.psum_scatter(
            d_qkv.astype(jnp.bfloat16), "shard", scatter_dimension=1, tiled=True
        ).astype(jnp.float32),
        lax.psum_scatter(
            d_bias.astype(jnp.bfloat16), "shard", scatter_dimension=1, tiled=True
        ).astype(jnp.float32),
        lax.psum_scatter(
            d_out_weight.astype(jnp.bfloat16), "shard", scatter_dimension=0, tiled=True
        ).astype(jnp.float32),
        lax.psum_scatter(
            d_ffn_gain.astype(jnp.bfloat16), "shard", scatter_dimension=0, tiled=True
        ).astype(jnp.float32),
        lax.psum_scatter(
            d_shared_gate_up.astype(jnp.bfloat16), "shard", scatter_dimension=1, tiled=True
        ).astype(jnp.float32),
        lax.psum_scatter(
            d_shared_down.astype(jnp.bfloat16), "shard", scatter_dimension=0, tiled=True
        ).astype(jnp.float32),
        lax.psum_scatter(
            d_shared_gate.astype(jnp.bfloat16), "shard", scatter_dimension=0, tiled=True
        ).astype(jnp.float32),
    )
    (
        sum_attn_gain,
        sum_qkv,
        sum_bias,
        sum_out,
        sum_ffn_gain,
        sum_shared_gate_up,
        sum_shared_down,
        sum_shared_gate,
        sum_expert_gate_up,
        sum_expert_down,
    ) = (
        lax.psum_scatter(
            part_attn_gain.astype(jnp.bfloat16), "rep", scatter_dimension=0, tiled=True
        ).astype(jnp.float32),
        lax.psum_scatter(
            part_qkv.astype(jnp.bfloat16), "rep", scatter_dimension=2, tiled=True
        ).astype(jnp.float32),
        lax.psum_scatter(
            part_bias.astype(jnp.bfloat16), "rep", scatter_dimension=1, tiled=True
        ).astype(jnp.float32),
        lax.psum_scatter(
            part_out.astype(jnp.bfloat16), "rep", scatter_dimension=1, tiled=True
        ).astype(jnp.float32),
        lax.psum_scatter(
            part_ffn_gain.astype(jnp.bfloat16), "rep", scatter_dimension=0, tiled=True
        ).astype(jnp.float32),
        lax.psum_scatter(
            part_shared_gate_up.astype(jnp.bfloat16), "rep", scatter_dimension=2, tiled=True
        ).astype(jnp.float32),
        lax.psum_scatter(
            part_shared_down.astype(jnp.bfloat16), "rep", scatter_dimension=1, tiled=True
        ).astype(jnp.float32),
        lax.psum_scatter(
            part_shared_gate.astype(jnp.bfloat16), "rep", scatter_dimension=0, tiled=True
        ).astype(jnp.float32),
        lax.psum_scatter(
            d_expert_gate_up.astype(jnp.bfloat16), "rep", scatter_dimension=2, tiled=True
        ).astype(jnp.float32),
        lax.psum_scatter(
            d_expert_down.astype(jnp.bfloat16), "rep", scatter_dimension=2, tiled=True
        ).astype(jnp.float32),
    )
    grad_attn_gain, grad_bias, grad_ffn_gain, grad_shared_gate = (
        lax.all_gather(sum_attn_gain, "rep", axis=0, tiled=True),
        lax.all_gather(sum_bias, "rep", axis=1, tiled=True),
        lax.all_gather(sum_ffn_gain, "rep", axis=0, tiled=True),
        lax.all_gather(sum_shared_gate, "rep", axis=0, tiled=True),
    )
    return (
        loss_value,
        out_rows.astype(jnp.bfloat16)[None],
        d_input_rows[None],
        grad_attn_gain,
        sum_qkv,
        grad_bias,
        sum_out,
        grad_ffn_gain,
        sum_shared_gate_up,
        sum_shared_down,
        grad_shared_gate,
        sum_expert_gate_up,
        sum_expert_down,
    )


def flip_pairs(count, bit):
    return [(place, place ^ bit) for place in range(count)]


def exchange(values, replicas, bit):
    return lax.ppermute(values, "rep", flip_pairs(replicas, bit))


def take_one(values, place, axis):
    return lax.dynamic_index_in_dim(values, place, axis, keepdims=False)


def add_low(first, second):
    return (first.astype(jnp.float32) + second.astype(jnp.float32)).astype(jnp.bfloat16)


def sum_over_chips(values, replicas, axis, row_first):
    place = lax.axis_index("rep")
    bits = (2, 4) if row_first else (4, 2)
    shape = values.shape
    values = values.reshape(shape[:axis] + (2, 2) + shape[axis + 1 :])
    if not row_first:
        values = jnp.swapaxes(values, axis, axis + 1)
    for bit, at in zip(bits, (axis + 1, axis)):
        mine = (place // bit) % 2
        kept = take_one(values, mine, at)
        values = add_low(kept, exchange(take_one(values, 1 - mine, at), replicas, bit))
    return values


def per_device_heads(
    tokens,
    teacher,
    valid_mask,
    block_mask,
    routes,
    gates,
    attn_gain,
    w_qkv,
    qkv_bias,
    w_out,
    ffn_gain,
    shared_gate_up,
    shared_down,
    shared_gate,
    expert_gate_up,
    expert_down,
):
    x_rows = tokens[0].astype(jnp.float32)
    row_count, model_width = x_rows.shape
    groups = lax.axis_size("shard")
    replicas = lax.axis_size("rep")
    halves = replicas // groups
    place = lax.axis_index("rep")
    group = lax.axis_index("shard")
    core = place % 2
    seq_len = row_count * replicas
    heads = HEADS // replicas
    head_cols = heads * HD
    slice_rows = w_qkv.shape[1]
    hidden_all = shared_gate_up.shape[2]
    hidden_cols = hidden_all // replicas
    out_cols = model_width // replicas
    score_scale = 1.0 / math.sqrt(HD)

    valid_rows = valid_mask[0].astype(jnp.float32)
    count_total = lax.psum(jnp.sum(valid_rows), ("rep", "shard"))

    vectors = jnp.concatenate(
        [attn_gain[None], ffn_gain[None], shared_gate[None], qkv_bias], axis=0
    )
    vectors = lax.all_gather(vectors, "shard", axis=1, tiled=True).astype(jnp.float32)
    attn_gain_float, ffn_gain_float, shared_gate_float = vectors[0], vectors[1], vectors[2]
    bias_float = lax.dynamic_slice_in_dim(vectors[3:], place * head_cols, head_cols, 1)

    qkv_weight = lax.all_gather(
        lax.dynamic_slice_in_dim(w_qkv, place * head_cols, head_cols, 2),
        "shard",
        axis=1,
        tiled=True,
    )
    normed_low = (x_rows * norm_scale(x_rows) * attn_gain_float).astype(jnp.bfloat16)
    normed_seq = lax.all_gather(normed_low, "rep", axis=0, tiled=True)

    down_part = shared_down.reshape(halves, replicas, -1, model_width)
    out_part = w_out.reshape(halves, replicas, -1, model_width)
    down_rows = down_part.shape[2]
    row_part = jnp.concatenate([take_one(down_part, place, 1), take_one(out_part, place, 1)], axis=1)
    row_part = lax.all_gather(row_part, "shard", axis=0, tiled=True)
    row_part = lax.all_to_all(row_part, "rep", split_axis=0, concat_axis=0, tiled=True)
    down_weight = row_part[:, :down_rows].reshape(-1, model_width)
    out_weight = row_part[:, down_rows:].reshape(-1, model_width)

    gate_up_weight = lax.all_gather(
        lax.dynamic_slice_in_dim(shared_gate_up, place * hidden_cols, hidden_cols, 2),
        "shard",
        axis=1,
        tiled=True,
    )

    projected = jnp.einsum(
        "ld,jdf->jlf", normed_seq, qkv_weight, preferred_element_type=jnp.float32
    )
    projected = projected + bias_float[:, None, :]
    cosine_table, sine_table = rope_tables(0, seq_len, HD)
    query_low = rotate(projected[0], cosine_table, sine_table, heads).astype(jnp.bfloat16)
    key_low = rotate(projected[1], cosine_table, sine_table, heads).astype(jnp.bfloat16)
    value_low = projected[2].astype(jnp.bfloat16)
    query_heads = query_low.reshape(seq_len, heads, HD)
    key_heads = key_low.reshape(seq_len, heads, HD)
    value_heads = value_low.reshape(seq_len, heads, HD)
    permitted = allowed_keys(block_mask[0], 0, seq_len, 0, seq_len, BLOCK)[None]
    scores = (
        jnp.einsum("qhd,khd->hqk", query_heads, key_heads, preferred_element_type=jnp.float32)
        * score_scale
    )
    scores = jnp.where(permitted, scores, NEG)
    terms = jnp.exp(scores - jnp.max(scores, axis=-1, keepdims=True))
    probs = terms / jnp.sum(terms, axis=-1, keepdims=True)
    probs_low = probs.astype(jnp.bfloat16)
    attended = jnp.einsum(
        "hqk,khd->qhd", probs_low, value_heads, preferred_element_type=jnp.float32
    )
    attended_low = attended.reshape(seq_len, head_cols).astype(jnp.bfloat16)
    branch = jnp.dot(attended_low, out_weight, preferred_element_type=jnp.float32)
    mid_rows = x_rows + lax.psum_scatter(
        branch.astype(jnp.bfloat16), "rep", scatter_dimension=0, tiled=True
    ).astype(jnp.float32)
    normed_mid = (mid_rows * norm_scale(mid_rows) * ffn_gain_float).astype(jnp.bfloat16)

    def gather_column(values):
        own = lax.all_gather(values, "shard", axis=0, tiled=False)
        return jnp.concatenate([own, exchange(own, replicas, 1)], axis=0)

    def scatter_column(parts):
        own = add_low(parts[:groups], exchange(parts[groups:], replicas, 1))
        return lax.psum_scatter(own, "shard", scatter_dimension=0, tiled=False)

    experts_total = groups * expert_gate_up.shape[0]
    route_weight = jnp.sum(
        jnp.where(
            routes[0][:, :, None] == jnp.arange(experts_total, dtype=jnp.int32),
            gates[0][:, :, None],
            0.0,
        ),
        axis=1,
    )
    column_weight = gather_column(route_weight)
    mine = group * 2 + core
    my_weight = take_one(column_weight, mine, 2)
    chosen = my_weight > 0
    slot = jnp.cumsum(chosen.astype(jnp.int32), axis=1) - 1
    pick = chosen[:, None, :] & (
        slot[:, None, :] == jnp.arange(CAP, dtype=jnp.int32)[None, :, None]
    )
    slot_weight = jnp.sum(jnp.where(pick, my_weight[:, None, :], 0.0), axis=2)
    pick_low = pick.astype(jnp.bfloat16)
    my_gate_up = take_one(expert_gate_up, core, 0)
    my_down = take_one(expert_down, core, 0)

    def to_slots(values):
        return jnp.einsum(
            "bst,btd->bsd", pick_low, values, preferred_element_type=jnp.float32
        ).astype(jnp.bfloat16)

    def from_slots(values):
        return jnp.einsum(
            "bst,bsd->btd", pick_low, values, preferred_element_type=jnp.float32
        ).astype(jnp.bfloat16)

    mid_column = gather_column(normed_mid)
    mid_seq = lax.all_gather(normed_mid, "rep", axis=0, tiled=True)

    expert_in = to_slots(mid_column).reshape(-1, model_width)
    expert_pre = jnp.einsum(
        "sd,jdf->jsf", expert_in, my_gate_up, preferred_element_type=jnp.float32
    )
    expert_hidden = swiglu(expert_pre[0], expert_pre[1]).astype(jnp.bfloat16)
    expert_out = jnp.dot(expert_hidden, my_down, preferred_element_type=jnp.float32)
    expert_out = expert_out.reshape(slot_weight.shape + (model_width,))
    expert_out = (slot_weight[:, :, None] * expert_out).astype(jnp.bfloat16)
    expert_mix = scatter_column(from_slots(expert_out))

    shared_pre = jnp.einsum(
        "ld,jdf->jlf", mid_seq, gate_up_weight, preferred_element_type=jnp.float32
    )
    shared_hidden = swiglu(shared_pre[0], shared_pre[1]).astype(jnp.bfloat16)
    shared_weight = jax.nn.sigmoid(
        jnp.sum(mid_seq.astype(jnp.float32) * shared_gate_float[None, :], axis=1)
    )
    shared_out = jnp.dot(shared_hidden, down_weight, preferred_element_type=jnp.float32)
    shared_mix = lax.psum_scatter(
        (shared_weight[:, None] * shared_out).astype(jnp.bfloat16),
        "rep",
        scatter_dimension=0,
        tiled=True,
    )

    out_rows = mid_rows + (shared_mix.astype(jnp.float32) + expert_mix.astype(jnp.float32))
    diff_rows = out_rows - teacher[0].astype(jnp.float32)
    squares_local = jnp.sum(valid_rows * jnp.sum(diff_rows * diff_rows, axis=1))
    tokens_all = row_count * replicas * groups
    d_rows = valid_rows[:, None] * diff_rows * (tokens_all / (2.0 * count_total))
    d_low = d_rows.astype(jnp.bfloat16)
    d_column = gather_column(d_low)
    d_seq = lax.all_gather(d_low, "rep", axis=0, tiled=True)

    d_expert_out = (slot_weight[:, :, None] * to_slots(d_column).astype(jnp.float32)).astype(
        jnp.bfloat16
    )
    d_expert_out = d_expert_out.reshape(-1, model_width)
    d_expert_hidden = jnp.einsum(
        "sd,fd->sf", d_expert_out, my_down, preferred_element_type=jnp.float32
    )
    d_gate_expert, d_up_expert = swiglu_grads(expert_pre[0], expert_pre[1], d_expert_hidden)
    d_expert_pre = jnp.stack([d_gate_expert, d_up_expert]).astype(jnp.bfloat16)
    d_expert_in = jnp.einsum(
        "jsf,jdf->sd", d_expert_pre, my_gate_up, preferred_element_type=jnp.float32
    ).astype(jnp.bfloat16)
    d_expert_in = d_expert_in.reshape(slot_weight.shape + (model_width,))
    d_mid_experts = scatter_column(from_slots(d_expert_in))

    d_shared_out = (shared_weight[:, None] * d_seq.astype(jnp.float32)).astype(jnp.bfloat16)
    d_plain_hidden = jnp.einsum(
        "ld,fd->lf", d_seq, down_weight, preferred_element_type=jnp.float32
    )
    d_logit = (
        jnp.sum(shared_hidden.astype(jnp.float32) * d_plain_hidden, axis=1)
        * shared_weight
        * (1.0 - shared_weight)
    )
    d_gate_shared, d_up_shared = swiglu_grads(
        shared_pre[0], shared_pre[1], shared_weight[:, None] * d_plain_hidden
    )
    d_shared_pre = jnp.stack([d_gate_shared, d_up_shared]).astype(jnp.bfloat16)
    d_mid_shared = jnp.einsum(
        "jlf,jdf->ld", d_shared_pre, gate_up_weight, preferred_element_type=jnp.float32
    )
    d_mid_shared = d_mid_shared + d_logit[:, None] * shared_gate_float[None, :]
    d_mid_shared = lax.psum_scatter(
        d_mid_shared.astype(jnp.bfloat16), "rep", scatter_dimension=0, tiled=True
    )

    d_gate_up_expert = jnp.einsum(
        "sd,jsf->jdf", expert_in, d_expert_pre, preferred_element_type=jnp.float32
    ).astype(jnp.bfloat16)
    d_down_expert = jnp.einsum(
        "sf,sd->fd", expert_hidden, d_expert_out, preferred_element_type=jnp.float32
    ).astype(jnp.bfloat16)
    d_shared_gate_up = jnp.einsum(
        "ld,jlf->jdf", mid_seq, d_shared_pre, preferred_element_type=jnp.float32
    ).astype(jnp.bfloat16)
    d_shared_down = jnp.einsum(
        "lf,ld->fd", shared_hidden, d_shared_out, preferred_element_type=jnp.float32
    ).astype(jnp.bfloat16)
    d_shared_gate = jnp.einsum("l,ld->d", d_logit, mid_seq.astype(jnp.float32))

    chips = replicas // 2
    expert_width = my_down.shape[0]
    cut = expert_width // 2
    grad_parts = (
        (d_gate_up_expert[0].reshape(chips, -1, expert_width), 0, True),
        (d_gate_up_expert[1].reshape(chips, -1, expert_width), 0, False),
        (d_down_expert[:cut].reshape(cut, chips, -1), 1, True),
        (d_down_expert[cut:].reshape(cut, chips, -1), 1, False),
    )
    grad_sums = [sum_over_chips(part, replicas, axis, first) for part, axis, first in grad_parts]

    def split_cores(values, axis):
        shape = values.shape
        values = values.reshape(shape[:axis] + (2, -1) + shape[axis + 1 :])
        kept = take_one(values, core, axis)
        other = exchange(take_one(values, 1 - core, axis), replicas, 1)
        low = jnp.where(core == 0, kept, other)
        high = jnp.where(core == 0, other, kept)
        return jnp.stack([low, high])

    grad_expert_gate_up = split_cores(jnp.stack(grad_sums[:2]), 1).astype(jnp.float32)
    grad_expert_down = split_cores(jnp.concatenate(grad_sums[2:], axis=0), 1).astype(jnp.float32)

    grad_shared_gate_up = lax.psum_scatter(
        d_shared_gate_up, "shard", scatter_dimension=1, tiled=True
    ).astype(jnp.float32)

    def row_grads(values):
        spread = lax.all_to_all(values, "rep", split_axis=1, concat_axis=0, tiled=True)
        return lax.psum_scatter(spread, "shard", scatter_dimension=0, tiled=True).astype(
            jnp.float32
        )

    grad_shared_down = row_grads(d_shared_down)

    d_normed_mid = d_mid_shared.astype(jnp.float32) + d_mid_experts.astype(jnp.float32)
    d_mid_norm, d_ffn_gain = norm_back(mid_rows, ffn_gain_float, d_normed_mid)
    d_mid = d_rows + d_mid_norm
    d_branch = lax.all_gather(d_mid.astype(jnp.bfloat16), "rep", axis=0, tiled=True)
    d_attended = jnp.einsum(
        "ld,fd->lf", d_branch, out_weight, preferred_element_type=jnp.float32
    )
    d_attended = d_attended.astype(jnp.bfloat16).reshape(seq_len, heads, HD)
    d_out_weight = jnp.einsum(
        "lf,ld->fd", attended_low, d_branch, preferred_element_type=jnp.float32
    ).astype(jnp.bfloat16)
    grad_out = row_grads(d_out_weight)

    d_values = jnp.einsum(
        "hqk,qhd->khd", probs_low, d_attended, preferred_element_type=jnp.float32
    )
    d_probs = jnp.einsum(
        "qhd,khd->hqk", d_attended, value_heads, preferred_element_type=jnp.float32
    )
    delta = jnp.sum(probs * d_probs, axis=-1, keepdims=True)
    d_scores = (probs * (d_probs - delta)).astype(jnp.bfloat16)
    d_query = jnp.einsum("hqk,khd->qhd", d_scores, key_heads, preferred_element_type=jnp.float32)
    d_keys = jnp.einsum("hqk,qhd->khd", d_scores, query_heads, preferred_element_type=jnp.float32)
    d_projected = jnp.stack(
        [
            rotate_back(
                d_query.reshape(seq_len, -1) * score_scale, cosine_table, sine_table, heads
            ),
            rotate_back(d_keys.reshape(seq_len, -1) * score_scale, cosine_table, sine_table, heads),
            d_values.reshape(seq_len, -1),
        ]
    ).astype(jnp.bfloat16)
    d_qkv = jnp.einsum(
        "ld,jlf->jdf", normed_seq, d_projected, preferred_element_type=jnp.float32
    ).astype(jnp.bfloat16)
    d_bias = jnp.sum(d_projected.astype(jnp.float32), axis=1)
    grad_qkv = lax.psum_scatter(d_qkv, "shard", scatter_dimension=1, tiled=True).astype(
        jnp.float32
    )
    d_normed_in = jnp.einsum(
        "jlf,jdf->ld", d_projected, qkv_weight, preferred_element_type=jnp.float32
    )
    d_normed_in = lax.psum_scatter(
        d_normed_in.astype(jnp.bfloat16), "rep", scatter_dimension=0, tiled=True
    ).astype(jnp.float32)
    d_x_norm, d_attn_gain = norm_back(x_rows, attn_gain_float, d_normed_in)
    d_input_rows = d_mid + d_x_norm

    d_bias_all = lax.dynamic_update_slice_in_dim(
        jnp.zeros((3, model_width), jnp.float32), d_bias, place * head_cols, 1
    )
    small = jnp.concatenate(
        [d_attn_gain[None], d_ffn_gain[None], d_shared_gate[None], d_bias_all], axis=0
    )
    small, squares_total = lax.psum((small, squares_local), ("rep", "shard"))
    small = lax.dynamic_slice_in_dim(small, group * slice_rows, slice_rows, 1)
    loss_value = squares_total / (count_total * model_width)
    return (
        loss_value,
        out_rows.astype(jnp.bfloat16)[None],
        d_input_rows[None],
        small[0],
        grad_qkv,
        small[3:],
        grad_out,
        small[1],
        grad_shared_gate_up,
        grad_shared_down,
        small[2],
        grad_expert_gate_up,
        grad_expert_down,
    )


def solution(mesh):
    by_heads = mesh.shape["rep"] == 8 and mesh.shape["shard"] == 4
    return jax.shard_map(
        per_device_heads if by_heads else per_device,
        mesh=mesh,
        in_specs=(
            P("shard", "rep", None),
            P("shard", "rep", None),
            P("shard", "rep"),
            P("shard", None, None),
            P("shard", "rep", None),
            P("shard", "rep", None),
            P("shard"),
            P(None, "shard", None),
            P(None, "shard"),
            P("shard", None),
            P("shard"),
            P(None, "shard", None),
            P("shard", None),
            P("shard"),
            P("shard", None, None, None),
            P("shard", None, None),
        ),
        out_specs=(
            P(),
            P("shard", "rep", None),
            P("shard", "rep", None),
            P("shard"),
            P(None, "shard", "rep"),
            P(None, "shard"),
            P("shard", "rep"),
            P("shard"),
            P(None, "shard", "rep"),
            P("shard", "rep"),
            P("shard"),
            P("shard", None, "rep", None),
            P("shard", None, "rep"),
        ),
        check_vma=False,
    )
```
